32 devices in a mesh: expert: 8 (over z, y), tensor: 4 (over x, core).
Axes of the slice: x: 2, y: 2, z: 4, core: 2. Of those that a mesh axis runs over, the one named last changes fastest.
Arguments:
- tokens: bfloat16 [1024, 768], P('expert', 'tensor'), may hold values from -6 to 6
- cotangent: bfloat16 [1024, 768], P('expert', 'tensor'), may hold values from -6 to 6
- attn_gain: bfloat16 [768], replicated, may hold values from 0.5 to 1.5
- qkv_weight: bfloat16 [3, 768, 768], P(None, None, 'tensor'), may hold values from -0.21875 to 0.21875
- out_weight: bfloat16 [768, 768], P('tensor'), may hold values from -0.875 to 0.875
- bias_table: float32 [32, 12], P(None, 'tensor'), may hold values from -6 to 6
- ffn_gain: bfloat16 [768], replicated, may hold values from 0.5 to 1.5
- router_weight: bfloat16 [768, 8], replicated, may hold values from -0.15625 to 0.15625
- expert_in: bfloat16 [8, 768, 3072], P('expert', None, 'tensor'), may hold values from -0.21875 to 0.21875
- expert_out: bfloat16 [8, 3072, 768], P('expert', 'tensor'), may hold values from -7 to 7
- routes: int32 [1024, 2], P('expert'), may hold values from 0 to 7, all different within a row; in each aligned block of 128 rows (0 to 127, 128 to 255, ...) at most 42 rows name the same one
- buckets: int32 [128], replicated, may hold values from 0 to 31, as said below
Outputs:
- mixed: bfloat16 [1024, 768], P('expert', 'tensor')
- tokens_grad: bfloat16 [1024, 768], P('expert', 'tensor')
- attn_gain_grad: float32 [768], replicated
- qkv_weight_grad: float32 [3, 768, 768], P(None, None, 'tensor')
- out_weight_grad: float32 [768, 768], P('tensor')
- bias_table_grad: float32 [32, 12], P(None, 'tensor')
- ffn_gain_grad: float32 [768], replicated
- router_weight_grad: float32 [768, 8], replicated
- expert_in_grad: float32 [8, 768, 3072], P('expert', None, 'tensor')
- expert_out_grad: float32 [8, 3072, 768], P('expert', 'tensor')
The draws below stay inside these ranges and needn't reach their ends.
Inputs may be any that keep to these rules, and one draw needn't show every extreme that they name: `routes`: each row names 2 different experts. Among the rows of one sequence no expert is named more than 42 times, and in some sequences one expert is named exactly 42 times. `buckets`: never falls as the distance grows; 0 at distance 0 and 31 at the largest distance.
All inputs are finite; a program needn't handle non-finite values.
Results may differ from the reference program's by a relative error of at most 0.024.
Values may be sent and summed in bfloat16 or wider, within the bound.
A program may use at most 64 MiB of HBM per device.

```python
import math
import jax
import jax.numpy as jnp
import numpy as np
from jax import lax

D = 768
HEADS = 12
HEAD = 64
FF = 3072
BUCKETS = 32
TOP = 2
TOK_DEV = 128
EXPERTS = 8
CAP = 42
TOKENS = 1024
N_EXPERT = 8
N_TENSOR = 4


def draw_buckets(key, part):
    key = jax.random.fold_in(key, 7)
    half_count = BUCKETS // 2
    shuffled = jax.random.permutation(key, TOK_DEV - half_count - 1) + half_count + 1
    breaks = shuffled[:half_count]
    distance = jnp.arange(TOK_DEV, dtype=jnp.int32)
    exact_part = jnp.minimum(distance, half_count - 1)
    passed = jnp.sum((breaks[None, :] <= distance[:, None]).astype(jnp.int32), axis=1)
    return (exact_part + passed).astype(jnp.int32)


def block_scale(rng, dims, pieces, smallest, top_value):
    def one(dim, shards_of):
        draws = jax.random.uniform(jax.random.fold_in(jax.random.fold_in(rng, 6), dim), (shards_of,), jnp.float32, smallest / len(pieces), top_value / len(pieces))
        return jnp.repeat(jnp.exp(draws), dims[dim] // shards_of).reshape((-1,) + (1,) * (len(dims) - dim - 1))

    loudness = one(*pieces[0])
    for cut in pieces[1:]:
        loudness = loudness * one(*cut)
    return loudness


def shared_out(own_key, own, number, rows, number_of, top, reach, skew):
    sequence = jax.random.permutation(own_key, number_of)
    packed, usual = load_shares(number_of, rows * top, reach, skew, True), load_shares(number_of, rows * top, reach, skew, False)
    places = jnp.arange(number_of)

    def named(sizes, turn):
        used = int((sizes > 0).sum())
        fixed = max(1, used // 4)
        moved = fixed + (places - fixed + turn * (used - fixed)) % max(1, number_of - fixed)
        return jnp.zeros((number_of,), jnp.int32).at[sequence[jnp.where(places < fixed, places, moved)]].set(jnp.asarray(sizes, jnp.int32))

    sizes = jnp.where(number % 4 == 0, named(packed, number // 4), named(usual, number - number // 4 - 1))
    mixed = jax.random.permutation(jax.random.fold_in(own, 3), number_of)
    donor, receiver = mixed[0:number_of // 2 * 2:2], mixed[1:number_of // 2 * 2:2]
    margin = jnp.minimum(sizes[donor] - 1, reach - sizes[receiver]) // 2
    margin = jnp.where((donor == sequence[0]) | (receiver == sequence[0]) | (sizes[receiver] == 0), 0, jnp.maximum(margin, 0))
    moved = jax.random.randint(jax.random.fold_in(own, 4), (number_of // 2,), 0, 1 << 20) % (margin + 1)
    sizes = sizes.at[donor].add(-moved).at[receiver].add(moved)
    items = jnp.searchsorted(jnp.cumsum(sizes), jnp.arange(rows * top), side="right").astype(jnp.int32)
    listing = items.reshape(top, rows).T
    listing = listing[jax.random.permutation(jax.random.fold_in(own, 1), rows)]
    turn = jax.random.randint(jax.random.fold_in(own, 2), (rows, 1), 0, top)
    return jnp.take_along_axis(listing, (jnp.arange(top)[None, :] + turn) % top, axis=1)


def load_shares(amount, total, most, skew, full):
    weights = [(1 << 20) // math.isqrt(standing ** skew) + 1 for standing in range(1, amount + 1)]
    largest = most if full else min(most, max(-(-total // amount), total * weights[0] // sum(weights)))
    least = 1 if total - largest >= amount - 1 else 0
    holding, surplus = [largest] + [least] * (amount - 1), total - largest - least * (amount - 1)
    while surplus > 0:
        candidates = [i for i in range(1, amount) if holding[i] < largest] or [i for i in range(1, amount) if holding[i] < most]
        pool, left = sum([weights[i] for i in candidates]), surplus
        for i in candidates:
            more = min(most - holding[i], max(1, left * weights[i] // pool), surplus)
            holding[i] = holding[i] + more
            surplus = surplus - more
    return np.array(holding)


def bell_draw(own_key, extent, width, limit, cuts=(), kind=jnp.bfloat16):
    loudness = block_scale(own_key, extent, cuts, -0.22, 0.18) if cuts else 1.0
    result = jax.random.normal(own_key, extent, jnp.float32) * width * loudness
    return jnp.minimum(jnp.maximum(result, -limit), limit).astype(kind)


def setup_inputs(seed: int = 0) -> dict:
    arg_keys = jax.random.split(jax.random.key(seed), 13)
    tokens = bell_draw(arg_keys[0], (TOKENS, D), 1.0, 6.0, ((0, 8), (1, 4)))
    cotangent = bell_draw(arg_keys[1], (TOKENS, D), 1.0, 6.0, ((0, 8), (1, 4)))
    attn_gain = jnp.clip(1.0 + 0.1 * jax.random.normal(arg_keys[2], (D,), jnp.float32), 0.5, 1.5).astype(jnp.bfloat16)
    qkv_weight = bell_draw(arg_keys[3], (3, D, HEADS * HEAD), D ** -0.5, 0.21875, ((2, 4),))
    out_weight = bell_draw(arg_keys[4], (HEADS * HEAD, D), (HEADS * HEAD // 16) ** -0.5, 0.875, ((0, 4),))
    bias_table = bell_draw(arg_keys[5], (BUCKETS, HEADS), 1.0, 6.0, ((1, 4),), jnp.float32)
    ffn_gain = jnp.clip(1.0 + 0.1 * jax.random.normal(arg_keys[6], (D,), jnp.float32), 0.5, 1.5).astype(jnp.bfloat16)
    router_weight = bell_draw(arg_keys[7], (D, EXPERTS), 0.027, 0.15625)
    expert_in = bell_draw(arg_keys[8], (EXPERTS, D, FF), D ** -0.5, 0.21875, ((0, 8), (2, 4)))
    expert_out = bell_draw(arg_keys[9], (EXPERTS, FF, D), 1.2, 7.0, ((0, 8), (1, 4)))
    routes_keys = jax.random.split(jax.random.fold_in(arg_keys[10], 1), TOKENS // TOK_DEV)
    routes_turns = jax.random.permutation(jax.random.fold_in(arg_keys[10], 3), TOKENS // TOK_DEV)
    routes = jax.vmap(lambda own, number: shared_out(jax.random.fold_in(arg_keys[10], 2), own, number, TOK_DEV, EXPERTS, TOP, CAP, 1))(routes_keys, routes_turns).reshape((TOKENS, TOP))
    buckets = draw_buckets(jax.random.fold_in(arg_keys[12], 71), 0)
    return {"tokens": tokens, "cotangent": cotangent, "attn_gain": attn_gain, "qkv_weight": qkv_weight, "out_weight": out_weight, "bias_table": bias_table, "ffn_gain": ffn_gain, "router_weight": router_weight, "expert_in": expert_in, "expert_out": expert_out, "routes": routes, "buckets": buckets}


PRECISE = lax.Precision.HIGHEST
EPSILON = 1e-06

@jax.custom_vjp
def low(v):
    return lax.optimization_barrier(v.astype(jnp.bfloat16)).astype(jnp.float32)

@jax.custom_vjp
def low_back(v):
    return v

def low_keep(v):
    return (low(v), None)

def low_pass(kept, grad):
    return (grad,)

def back_keep(v):
    return (v, None)

def back_low(kept, grad):
    return (low(grad),)
low.defvjp(low_keep, low_pass)
low_back.defvjp(back_keep, back_low)

def rms_norm(values, norm_gain):
    factor = lax.rsqrt(lax.optimization_barrier(jnp.mean(values * values, axis=-1, keepdims=True)) + EPSILON)
    return low(values * factor * norm_gain)

def destinations(routes):
    paired = routes.reshape(N_EXPERT, TOK_DEV * TOP)
    onehot = (paired[:, :, None] == jnp.arange(EXPERTS, dtype=jnp.int32)[None, None, :]).astype(jnp.int32)
    earlier = (jnp.cumsum(onehot, axis=1) - onehot).astype(jnp.int32)
    slots = lax.optimization_barrier(jnp.sum(earlier * onehot, axis=-1)).astype(jnp.int32)
    source = jnp.arange(N_EXPERT, dtype=jnp.int32)[:, None]
    return (paired * (N_EXPERT * CAP) + source * CAP + slots).reshape(-1).astype(jnp.int32)

def expert_block(blocks):
    rows, w_first, w_second = blocks
    group_size = FF // N_TENSOR
    summed = jnp.zeros((rows.shape[0], D), jnp.float32)
    for group in range(N_TENSOR):
        shared = low_back(rows)
        hidden = low_back(jnp.dot(shared, w_first[:, group * group_size:(group + 1) * group_size], precision=PRECISE))
        active = low(jax.nn.gelu(hidden, approximate=False))
        partial_out = jnp.dot(active, w_second[group * group_size:(group + 1) * group_size], precision=PRECISE)
        summed = summed + low_back(low(partial_out))
    return summed

def forward(tokens, attn_gain, qkv_weight, out_weight, bias_table, ffn_gain, router_weight, expert_in, expert_out, routes, buckets):
    normed = rms_norm(tokens, attn_gain)
    projected = [low_back(low(jnp.dot(normed, qkv_weight[member], precision=PRECISE))) for member in range(3)]
    shaped = [item.reshape(N_EXPERT, TOK_DEV, HEADS, HEAD) for item in projected]
    position = jnp.arange(TOK_DEV, dtype=jnp.int32)
    spacing = position[:, None] - position[None, :]
    causal = spacing >= 0
    distance_bias = bias_table[buckets]
    full_bias = jnp.transpose(distance_bias[jnp.maximum(spacing, 0)], (2, 0, 1))

    def attend(blocks):
        queries, keys_in, values_in = blocks
        scores = jnp.einsum('qhd,khd->hqk', queries, keys_in, precision=PRECISE) * 0.125 + full_bias
        scores = low_back(scores)
        scores = jnp.where(causal[None], scores, -1e+30)
        weights = low(jax.nn.softmax(scores, axis=-1))
        context = jnp.einsum('hqk,khd->qhd', weights, values_in, precision=PRECISE)
        return low_back(low(context)).reshape(TOK_DEV, HEADS * HEAD)
    context = lax.map(jax.checkpoint(attend), (shaped[0], shaped[1], shaped[2])).reshape(TOKENS, HEADS * HEAD)
    attended = low_back(jnp.dot(context, out_weight, precision=PRECISE))
    residual = tokens + attended
    ffn_in = rms_norm(residual, ffn_gain)
    logits = low_back(jnp.dot(ffn_in, router_weight, precision=PRECISE))
    router_probs = jax.nn.softmax(logits, axis=-1)
    gate_values = jnp.take_along_axis(router_probs, routes, axis=1)
    targets = destinations(routes)
    buffer = jnp.zeros((EXPERTS * N_EXPERT * CAP, D), jnp.float32).at[targets].set(jnp.repeat(ffn_in, TOP, axis=0))
    outputs = lax.map(jax.checkpoint(expert_block), (buffer.reshape(EXPERTS, N_EXPERT * CAP, D), expert_in, expert_out))
    gathered = outputs.reshape(EXPERTS * N_EXPERT * CAP, D)[targets].reshape(TOKENS, TOP, D)
    return residual + lax.optimization_barrier(jnp.sum(gate_values[:, :, None] * gathered, axis=1))

def reference(tokens, cotangent, attn_gain, qkv_weight, out_weight, bias_table, ffn_gain, router_weight, expert_in, expert_out, routes, buckets):
    floats = tuple((array_in.astype(jnp.float32) for array_in in (tokens, attn_gain, qkv_weight, out_weight, bias_table, ffn_gain, router_weight, expert_in, expert_out)))

    def wrapped(*values):
        return forward(*values, routes, buckets)
    mixed, pullback = jax.vjp(wrapped, *floats)
    gradients = pullback(cotangent.astype(jnp.float32))
    return (mixed.astype(jnp.bfloat16), gradients[0].astype(jnp.bfloat16), gradients[1], gradients[2], gradients[3], gradients[4], gradients[5], gradients[6], gradients[7], gradients[8])
```

```python
import functools

import jax
import jax.numpy as jnp
from jax import lax
from jax.experimental import pallas as pl
from jax.experimental.pallas import tpu as pltpu
from jax.sharding import PartitionSpec as P

PRECISE = lax.Precision.HIGHEST
EPSILON = 1e-06
ROOT_HALF = 0.7071067811865476
INV_ROOT_TAU = 0.3989422804014327
F32 = jnp.float32
BF16 = jnp.bfloat16
MESH = pl.DeviceIdType.MESH


def exchange_kernel(plan, n_expert, n_tensor, *refs):
    count = len(plan)
    sources, results, sems = refs[:count], refs[count : 2 * count], refs[2 * count :]
    my_e, my_t = lax.axis_index("expert"), lax.axis_index("tensor")
    sizes = {"expert": n_expert, "tensor": n_tensor, "all": n_expert * n_tensor}

    def device_at(scope, step):
        if scope == "tensor":
            return my_e, lax.rem(my_t + step, n_tensor)
        if scope == "expert":
            return lax.rem(my_e + step, n_expert), my_t
        place = lax.rem(my_e * n_tensor + my_t + step, n_expert * n_tensor)
        return place // n_tensor, lax.rem(place, n_tensor)

    def slot_of(scope, e, t):
        return {"expert": (e,), "tensor": (t,), "all": (e, t)}[scope]

    def number_of(scope, e, t):
        return {"expert": e, "tensor": t, "all": e * n_tensor + t}[scope]

    scopes = []
    for scope, _ in plan:
        if scope not in scopes:
            scopes.append(scope)
    if "all" in scopes:
        scopes = ["all"]
    barrier = pltpu.get_barrier_semaphore()
    for scope in scopes:

        def greet(step, carry, scope=scope):
            pl.semaphore_signal(barrier, inc=1, device_id=device_at(scope, step), device_id_type=MESH)
            return carry

        lax.fori_loop(1, sizes[scope], greet, 0)
    pl.semaphore_wait(barrier, sum(sizes[scope] - 1 for scope in scopes))

    def copy_of(k, step, back):
        scope, kind = plan[k]
        e, t = device_at(scope, step)
        source = sources[k]
        if kind == "split":
            source = source.at[slot_of(scope, e, t)]
        if back:
            e2, t2 = device_at(scope, sizes[scope] - step)
            place, number = slot_of(scope, e2, t2), number_of(scope, e2, t2)
        else:
            place, number = slot_of(scope, my_e, my_t), number_of(scope, my_e, my_t)
        return pltpu.make_async_remote_copy(
            src_ref=source,
            dst_ref=results[k].at[place],
            send_sem=sems[3 * k].at[number_of(scope, e, t)],
            recv_sem=sems[3 * k + 1].at[number],
            device_id=(e, t),
            device_id_type=MESH,
        )

    own = []
    for k, (scope, kind) in enumerate(plan):

        def start(step, carry, k=k):
            copy_of(k, step, False).start()
            return carry

        lax.fori_loop(1, sizes[scope], start, 0)
        mine = slot_of(scope, my_e, my_t)
        source = sources[k].at[mine] if kind == "split" else sources[k]
        copy = pltpu.make_async_copy(source, results[k].at[mine], sems[3 * k + 2])
        copy.start()
        own.append(copy)
    for k, (scope, kind) in enumerate(plan):

        def finish(step, carry, k=k):
            copy_of(k, step, False).wait_send()
            copy_of(k, step, True).wait_recv()
            return carry

        lax.fori_loop(1, sizes[scope], finish, 0)
        own[k].wait()


def exchange(number, *moves):
    n_expert, n_tensor = lax.axis_size("expert"), lax.axis_size("tensor")
    lead = {"expert": (n_expert,), "tensor": (n_tensor,), "all": (n_expert, n_tensor)}
    plan = tuple((scope, kind) for scope, kind, _ in moves)
    arrays = [array for _, _, array in moves]
    shapes, scratch = [], []
    for scope, kind, array in moves:
        shape = array.shape if kind == "split" else lead[scope] + array.shape
        shapes.append(jax.ShapeDtypeStruct(shape, array.dtype))
        amount = 1
        for size in lead[scope]:
            amount *= size
        scratch += [
            pltpu.SemaphoreType.DMA((amount,)),
            pltpu.SemaphoreType.DMA((amount,)),
            pltpu.SemaphoreType.DMA,
        ]
    return pl.pallas_call(
        functools.partial(exchange_kernel, plan, n_expert, n_tensor),
        out_shape=tuple(shapes),
        in_specs=[pl.BlockSpec(memory_space=pl.ANY)] * len(arrays),
        out_specs=tuple([pl.BlockSpec(memory_space=pl.ANY)] * len(arrays)),
        scratch_shapes=scratch,
        compiler_params=pltpu.CompilerParams(collective_id=number, has_side_effects=True),
    )(*arrays)


def gelu_slope(values):
    return (
        0.5 * (1.0 + lax.erf(values * ROOT_HALF))
        + values * jnp.exp(-0.5 * values * values) * INV_ROOT_TAU
    )


def diagonal_sums(grid):
    heads_here, length, _ = grid.shape
    flipped = grid[:, :, ::-1]
    padded = jnp.concatenate([flipped, jnp.zeros_like(flipped)], axis=2).reshape(heads_here, -1)
    window = lax.slice_in_dim(padded, length - 1, length - 1 + length * (2 * length - 1), axis=1)
    window = window.reshape(heads_here, length, 2 * length - 1)
    return jnp.sum(window[:, :, :length], axis=1)


def spread_diagonals(rows):
    heads_here, length = rows.shape
    period = jnp.concatenate(
        [rows[:, :1], jnp.zeros((heads_here, length), F32), rows[:, :0:-1]], axis=1
    )
    flat = jnp.tile(period, (1, length))[:, : length * (2 * length - 1)]
    return flat.reshape(heads_here, length, 2 * length - 1)[:, :, :length]


def two_parts(values):
    high = lax.reduce_precision(values, 8, 7)
    return high.astype(BF16), (values - high).astype(BF16)


def dot(a, b, dims):
    return lax.dot_general(a, b, (dims, ((), ())), preferred_element_type=F32)


def per_device(
    tokens,
    cotangent,
    attn_gain,
    qkv_weight,
    out_weight,
    bias_table,
    ffn_gain,
    router_weight,
    expert_in,
    expert_out,
    routes,
    buckets,
):
    n_expert, n_tensor = lax.axis_size("expert"), lax.axis_size("tensor")
    tensor_index = lax.axis_index("tensor")
    seq_len, share = tokens.shape
    width = share * n_tensor
    heads_here = bias_table.shape[1]
    local = qkv_weight.shape[2]
    head_size = local // heads_here
    experts = router_weight.shape[1]
    top_count = routes.shape[1]
    capacity = 4 * top_count * seq_len // (3 * experts)
    rows_each = -(-(capacity + 2) // 16) * 16
    all_rows = experts * rows_each

    (both,) = exchange(0, ("tensor", "whole", jnp.concatenate([tokens, cotangent], axis=1)))
    both = both.transpose(1, 0, 2)
    inputs = both[:, :, :share].reshape(seq_len, width).astype(F32)
    whole_cot = both[:, :, share:].reshape(seq_len, width)
    grad_out = whole_cot.astype(F32)

    expert_ids = jnp.arange(experts, dtype=jnp.int32)
    chosen = routes[:, :, None] == expert_ids[None, None, :]
    paired = routes.reshape(-1)
    pair_hot = (paired[:, None] == expert_ids[None, :]).astype(F32)
    order = jnp.arange(seq_len * top_count, dtype=jnp.int32)
    before = (order[:, None] > order[None, :]).astype(BF16)
    earlier = dot(before, pair_hot.astype(BF16), ((1,), (0,)))
    slots = jnp.sum(earlier * pair_hot, axis=-1).astype(jnp.int32)
    target_pairs = (paired * rows_each + slots).reshape(seq_len, top_count)
    back_pairs = (paired * (n_tensor * rows_each) + slots).reshape(seq_len, top_count)
    columns = jnp.arange(all_rows, dtype=jnp.int32)
    picks = [target_pairs[:, k : k + 1] == columns[None, :] for k in range(top_count)]
    pick_all = sum([pick.astype(BF16) for pick in picks])
    cot_rows = dot(pick_all, whole_cot, ((0,), (0,))).astype(BF16)

    r_first = lax.rsqrt(jnp.mean(inputs * inputs, axis=-1, keepdims=True) + EPSILON)
    normed = (inputs * r_first * attn_gain.astype(F32)).astype(BF16)
    projected = jnp.einsum("td,cdf->ctf", normed, qkv_weight, preferred_element_type=F32).astype(BF16)
    queries = projected[0].reshape(seq_len, heads_here, head_size)
    keys_here = projected[1].reshape(seq_len, heads_here, head_size)
    values_here = projected[2].reshape(seq_len, heads_here, head_size)
    position = jnp.arange(seq_len, dtype=jnp.int32)
    causal = position[:, None] >= position[None, :]
    bucket_hot = (
        buckets[:, None] == jnp.arange(bias_table.shape[0], dtype=jnp.int32)[None, :]
    ).astype(F32)
    bias_rows = jnp.einsum("bh,tb->ht", bias_table, bucket_hot, precision=PRECISE)
    full_bias = spread_diagonals(bias_rows)
    raw_scores = (
        jnp.einsum("qhd,khd->hqk", queries, keys_here, preferred_element_type=F32) * 0.125 + full_bias
    )
    scores = jnp.where(causal[None], raw_scores, -1e30)
    row_max = jnp.max(scores, axis=-1, keepdims=True)
    powers = jnp.exp(scores - row_max)
    soft = powers / jnp.sum(powers, axis=-1, keepdims=True)
    weights = soft.astype(BF16)
    context = jnp.einsum("hqk,khd->qhd", weights, values_here, preferred_element_type=F32)
    context = context.astype(BF16).reshape(seq_len, local)

    whole_context, whole_out, cot_recv = exchange(
        1,
        ("tensor", "whole", context),
        ("tensor", "whole", out_weight),
        ("expert", "split", cot_rows.reshape(n_expert, rows_each, width)),
    )
    attended = dot(
        whole_context.transpose(1, 0, 2).reshape(seq_len, width),
        whole_out.reshape(width, width),
        ((1,), (0,)),
    )
    residual = inputs + attended
    r_second = lax.rsqrt(jnp.mean(residual * residual, axis=-1, keepdims=True) + EPSILON)
    ffn_in = (residual * r_second * ffn_gain.astype(F32)).astype(BF16)
    router_probs = jax.nn.softmax(dot(ffn_in, router_weight, ((1,), (0,))), axis=-1)
    gate_values = jnp.sum(jnp.where(chosen, router_probs[:, None, :], 0.0), axis=-1)
    slot_gate = sum(
        [
            jnp.sum(jnp.where(picks[k], gate_values[:, k : k + 1], 0.0), axis=0)
            for k in range(top_count)
        ]
    ).reshape(n_expert, rows_each)
    line = jnp.arange(rows_each, dtype=jnp.int32)

    def add_lines(body, values):
        extra = body.ndim - 3
        high, low = [
            jnp.pad(part, ((0, 0), (0, body.shape[-1] - rows_each))).reshape(
                (n_expert,) + (1,) * (extra + 1) + (body.shape[-1],)
            )
            for part in two_parts(values)
        ]
        at = line[:, None]
        return jnp.where(at == capacity, high, jnp.where(at == capacity + 1, low, body))

    def read_lines(body):
        return (
            body[..., capacity, :rows_each].astype(F32)
            + body[..., capacity + 1, :rows_each].astype(F32)
        )

    send_rows = dot(pick_all, ffn_in, ((0,), (0,))).astype(BF16).reshape(n_expert, rows_each, width)
    (received,) = exchange(2, ("expert", "split", add_lines(send_rows, slot_gate)))
    row_gate = read_lines(received).reshape(all_rows, 1)
    kept_rows = jnp.where((line < capacity)[None, :, None], received, 0).reshape(all_rows, width)
    w_in, w_out = expert_in[0], expert_out[0]
    hidden = dot(kept_rows, w_in, ((1,), (0,)))
    active = jax.nn.gelu(hidden, approximate=False).astype(BF16)
    part_out = dot(active, w_out, ((1,), (0,))).astype(BF16)
    cot_here = cot_recv.reshape(all_rows, width).astype(F32)
    grad_part = (row_gate * cot_here).astype(BF16)
    grad_active = dot(grad_part, w_out, ((1,), (1,)))
    grad_hidden = (grad_active * gelu_slope(hidden)).astype(BF16)
    grad_rows = dot(grad_hidden, w_in, ((1,), (1,))).astype(BF16)
    row_dots = jnp.sum(part_out.astype(F32) * cot_here, axis=-1).reshape(n_expert, rows_each)
    expert_out_grad = dot(active, grad_part, ((0,), (0,)))[None]
    expert_in_grad = dot(kept_rows, grad_hidden, ((0,), (0,)))[None]

    back = jnp.concatenate(
        [
            part_out.reshape(n_expert, rows_each, n_tensor, share),
            grad_rows.reshape(n_expert, rows_each, n_tensor, share),
        ],
        axis=-1,
    ).transpose(0, 2, 1, 3)
    (returned,) = exchange(3, ("all", "split", add_lines(back, row_dots)))
    slot_dots = jnp.sum(read_lines(returned), axis=1).reshape(1, all_rows)
    grad_gates = jnp.stack(
        [jnp.sum(jnp.where(picks[k], slot_dots, 0.0), axis=-1) for k in range(top_count)], axis=-1
    )
    places = jnp.arange(n_tensor * all_rows, dtype=jnp.int32)
    group_start = places - (places // rows_each % n_tensor) * rows_each
    back_pick = jnp.concatenate(
        [back_pairs[:, k : k + 1] == group_start[None, :] for k in range(top_count)], axis=0
    ).astype(BF16)
    picked = dot(back_pick, returned.reshape(n_tensor * all_rows, 2 * share), ((1,), (0,)))
    picked = picked.reshape(top_count, seq_len, 2 * share)
    expert_share = sum([gate_values[:, k : k + 1] * picked[k, :, :share] for k in range(top_count)])
    residual_share = lax.dynamic_slice_in_dim(residual, tensor_index * share, share, 1)
    mixed = (residual_share + expert_share).astype(BF16)

    grad_ffn_share = jnp.sum(picked[:, :, share:], axis=0).astype(BF16)
    (grad_ffn_experts,) = exchange(4, ("tensor", "whole", grad_ffn_share))
    grad_ffn_experts = grad_ffn_experts.transpose(1, 0, 2).reshape(seq_len, width).astype(F32)
    grad_probs = jnp.sum(jnp.where(chosen, grad_gates[:, :, None], 0.0), axis=1)
    grad_logits = (
        router_probs * (grad_probs - jnp.sum(router_probs * grad_probs, axis=-1, keepdims=True))
    ).astype(BF16)
    router_grad = dot(grad_logits, ffn_in, ((0,), (0,)))
    grad_ffn_in = grad_ffn_experts + dot(grad_logits, router_weight, ((1,), (1,)))
    ffn_gain_grad = jnp.sum(grad_ffn_in * residual * r_second, axis=0)
    scaled_second = grad_ffn_in * ffn_gain.astype(F32)
    grad_residual = (
        grad_out
        + r_second * scaled_second
        - residual * r_second**3 * jnp.mean(scaled_second * residual, axis=-1, keepdims=True)
    )
    grad_attended = grad_residual.astype(BF16)
    grad_context = dot(grad_attended, out_weight, ((1,), (1,))).astype(BF16)
    grad_context = grad_context.reshape(seq_len, heads_here, head_size)
    grad_values = jnp.einsum("hqk,qhd->khd", weights, grad_context, preferred_element_type=F32)
    grad_weights = jnp.einsum("qhd,khd->hqk", grad_context, values_here, preferred_element_type=F32)
    grad_scores = (
        soft * (grad_weights - jnp.sum(soft * grad_weights, axis=-1, keepdims=True))
    ).astype(BF16)
    grad_queries = jnp.einsum("hqk,khd->qhd", grad_scores, keys_here, preferred_element_type=F32) * 0.125
    grad_keys = jnp.einsum("hqk,qhd->khd", grad_scores, queries, preferred_element_type=F32) * 0.125
    distance_grad = diagonal_sums(grad_scores.astype(F32))
    table_grad = jnp.einsum("tb,ht->bh", bucket_hot, distance_grad, precision=PRECISE)
    grad_projected = jnp.concatenate(
        [part.astype(BF16).reshape(seq_len, local) for part in (grad_queries, grad_keys, grad_values)],
        axis=1,
    )
    qkv_flat = qkv_weight.transpose(1, 0, 2).reshape(width, 3 * local)
    grad_normed_part = dot(grad_projected, qkv_flat, ((1,), (1,)))
    qkv_grad = dot(normed, grad_projected, ((0,), (0,)))
    out_grad = dot(grad_attended, context, ((0,), (0,)))
    attn_part = jnp.sum(grad_normed_part * inputs * r_first, axis=0)
    row_part = jnp.sum(grad_normed_part * attn_gain.astype(F32) * inputs, axis=-1, keepdims=True)
    row_high, row_low = two_parts(row_part)
    shares = grad_normed_part.astype(BF16).reshape(seq_len, n_tensor, share).transpose(1, 0, 2)
    pad = (-share - 2) % 128
    tail = jnp.concatenate([row_high, row_low, jnp.zeros((seq_len, pad), BF16)], axis=1)
    shares = jnp.concatenate(
        [shares, jnp.broadcast_to(tail[None], (n_tensor,) + tail.shape)], axis=2
    )
    table_line = jnp.pad(table_grad.reshape(1, -1), ((0, 0), (0, width - table_grad.size)))
    pack = jnp.concatenate([attn_part[None], ffn_gain_grad[None], table_line, router_grad], axis=0)
    pack = jnp.pad(pack, ((0, -pack.shape[0] % 8), (0, 0)))
    grads = jnp.concatenate([qkv_grad, out_grad], axis=1)
    block = width // n_expert
    if block % 16 == 0:
        blocks, packs, normed_parts = exchange(
            5,
            ("expert", "split", grads.astype(BF16).reshape(n_expert, block, -1)),
            ("expert", "whole", pack),
            ("tensor", "split", shares),
        )
        block_sum = jnp.sum(blocks.astype(F32), axis=0).astype(BF16)
    else:
        packs, normed_parts = exchange(
            5, ("expert", "whole", pack), ("tensor", "split", shares)
        )
    pack = jnp.sum(packs, axis=0)
    attn_rows = jnp.pad(pack[:1], ((0, 7), (0, 0)))
    if block % 16 == 0:
        grads, attn_rows = exchange(
            6, ("expert", "whole", block_sum), ("tensor", "whole", attn_rows)
        )
        grads = grads.reshape(width, -1).astype(F32)
    else:
        (attn_rows,) = exchange(6, ("tensor", "whole", attn_rows))
        grads = lax.psum(grads, "expert")
    attn_gain_grad = jnp.sum(attn_rows[:, 0], axis=0)
    normed_sum = jnp.sum(normed_parts.astype(F32), axis=0)
    row_mean = (normed_sum[:, share : share + 1] + normed_sum[:, share + 1 : share + 2]) / width

    def own_share(values):
        return lax.dynamic_slice_in_dim(values, tensor_index * share, share, values.ndim - 1)

    own_inputs = tokens.astype(F32)
    tokens_grad = (
        own_share(grad_residual)
        + r_first * (normed_sum[:, :share] * own_share(attn_gain.astype(F32)))
        - own_inputs * r_first**3 * row_mean
    ).astype(BF16)
    qkv_out = grads[:, : 3 * local].reshape(width, 3, local).transpose(1, 0, 2)
    return (
        mixed,
        tokens_grad,
        attn_gain_grad,
        qkv_out,
        grads[:, 3 * local :].T,
        pack[2, : table_grad.size].reshape(table_grad.shape),
        pack[1],
        pack[3 : 3 + experts].T,
        expert_in_grad,
        expert_out_grad,
    )


def solution(mesh):
    placed = (
        P("expert", "tensor"),
        P("expert", "tensor"),
        P(),
        P(None, None, "tensor"),
        P("tensor", None),
        P(None, "tensor"),
        P(),
        P(),
        P("expert", None, "tensor"),
        P("expert", "tensor", None),
        P("expert", None),
        P(),
    )
    return jax.shard_map(
        per_device,
        mesh=mesh,
        in_specs=placed,
        out_specs=(
            P("expert", "tensor"),
            P("expert", "tensor"),
            P(),
            P(None, None, "tensor"),
            P("tensor", None),
            P(None, "tensor"),
            P(),
            P(),
            P("expert", None, "tensor"),
            P("expert", "tensor", None),
        ),
        check_vma=False,
    )
```

```python
import functools

import jax
import jax.numpy as jnp
from jax import lax
from jax.experimental import pallas as pl
from jax.experimental.pallas import tpu as pltpu
from jax.sharding import PartitionSpec as P

PRECISE = lax.Precision.HIGHEST
EPSILON = 1e-06
ROOT_HALF = 0.7071067811865476
INV_ROOT_TAU = 0.3989422804014327
F32 = jnp.float32
BF16 = jnp.bfloat16
MESH = pl.DeviceIdType.MESH


def exchange_kernel(plan, n_expert, n_tensor, *refs):
    count = len(plan)
    sources, results, sems = refs[:count], refs[count : 2 * count], refs[2 * count :]
    my_e, my_t = lax.axis_index("expert"), lax.axis_index("tensor")
    sizes = {"expert": n_expert, "tensor": n_tensor, "all": n_expert * n_tensor}

    def device_at(scope, step):
        if scope == "tensor":
            return my_e, lax.rem(my_t + step, n_tensor)
        if scope == "expert":
            return lax.rem(my_e + step, n_expert), my_t
        place = lax.rem(my_e * n_tensor + my_t + step, n_expert * n_tensor)
        return place // n_tensor, lax.rem(place, n_tensor)

    def slot_of(scope, e, t):
        return {"expert": (e,), "tensor": (t,), "all": (e, t)}[scope]

    def number_of(scope, e, t):
        return {"expert": e, "tensor": t, "all": e * n_tensor + t}[scope]

    scopes = []
    for scope, _ in plan:
        if scope not in scopes:
            scopes.append(scope)
    if "all" in scopes:
        scopes = ["all"]
    barrier = pltpu.get_barrier_semaphore()
    for scope in scopes:

        def greet(step, carry, scope=scope):
            pl.semaphore_signal(barrier, inc=1, device_id=device_at(scope, step), device_id_type=MESH)
            return carry

        lax.fori_loop(1, sizes[scope], greet, 0)
    pl.semaphore_wait(barrier, sum(sizes[scope] - 1 for scope in scopes))

    def copy_of(k, step, back):
        scope, kind = plan[k]
        e, t = device_at(scope, step)
        source = sources[k]
        if kind == "split":
            source = source.at[slot_of(scope, e, t)]
        if back:
            e2, t2 = device_at(scope, sizes[scope] - step)
            place, number = slot_of(scope, e2, t2), number_of(scope, e2, t2)
        else:
            place, number = slot_of(scope, my_e, my_t), number_of(scope, my_e, my_t)
        return pltpu.make_async_remote_copy(
            src_ref=source,
            dst_ref=results[k].at[place],
            send_sem=sems[3 * k].at[number_of(scope, e, t)],
            recv_sem=sems[3 * k + 1].at[number],
            device_id=(e, t),
            device_id_type=MESH,
        )

    def relay_of(k, step, stage):
        scope = plan[k][0]
        half = sizes[scope] // 2
        me = my_e if scope == "expert" else my_t
        high, low = me // 2, lax.rem(me, 2)
        other = 1 - low
        after = lax.rem(high + step, half)
        before = lax.rem(high + half - step, half)
        target, origin, number = {
            "out": (after * 2 + low, me, after * 2 + low),
            "in": (after * 2 + low, before * 2 + low, 0),
            "pair": (high * 2 + other, me, high * 2 + other),
            "on": (high * 2 + other, before * 2 + low, before * 2 + other),
            "over": (high * 2 + other, before * 2 + other, 0),
        }[stage]
        return pltpu.make_async_remote_copy(
            src_ref=results[k].at[origin] if stage == "on" else sources[k],
            dst_ref=results[k].at[origin],
            send_sem=sems[3 * k].at[number],
            recv_sem=sems[3 * k + 1].at[origin],
            device_id=(target, my_t) if scope == "expert" else (my_e, target),
            device_id_type=MESH,
        )

    def steps(k, stage, act, first=1):
        def one(step, carry):
            getattr(relay_of(k, step, stage), act)()
            return carry

        lax.fori_loop(first, sizes[plan[k][0]] // 2, one, 0)

    own = []
    for k, (scope, kind) in enumerate(plan):

        def start(step, carry, k=k):
            copy_of(k, step, False).start()
            return carry

        if kind == "relay":
            steps(k, "out", "start")
            relay_of(k, 0, "pair").start()
        else:
            lax.fori_loop(1, sizes[scope], start, 0)
        mine = slot_of(scope, my_e, my_t)
        source = sources[k].at[mine] if kind == "split" else sources[k]
        copy = pltpu.make_async_copy(source, results[k].at[mine], sems[3 * k + 2])
        copy.start()
        own.append(copy)
    for k, (scope, kind) in enumerate(plan):
        if kind == "relay":

            def pass_on(step, carry, k=k):
                relay_of(k, step, "in").wait_recv()
                relay_of(k, step, "on").start()
                return carry

            lax.fori_loop(1, sizes[scope] // 2, pass_on, 0)
    for k, (scope, kind) in enumerate(plan):

        def finish(step, carry, k=k):
            copy_of(k, step, False).wait_send()
            copy_of(k, step, True).wait_recv()
            return carry

        if kind == "relay":
            steps(k, "out", "wait_send")
            relay_of(k, 0, "pair").wait_send()
            steps(k, "on", "wait_send")
            steps(k, "over", "wait_recv", 0)
        else:
            lax.fori_loop(1, sizes[scope], finish, 0)
        own[k].wait()


def exchange(number, *moves):
    n_expert, n_tensor = lax.axis_size("expert"), lax.axis_size("tensor")
    lead = {"expert": (n_expert,), "tensor": (n_tensor,), "all": (n_expert, n_tensor)}
    plan = tuple((scope, kind) for scope, kind, _ in moves)
    arrays = [array for _, _, array in moves]
    shapes, scratch = [], []
    for scope, kind, array in moves:
        shape = array.shape if kind == "split" else lead[scope] + array.shape
        shapes.append(jax.ShapeDtypeStruct(shape, array.dtype))
        amount = 1
        for size in lead[scope]:
            amount *= size
        scratch += [
            pltpu.SemaphoreType.DMA((amount,)),
            pltpu.SemaphoreType.DMA((amount,)),
            pltpu.SemaphoreType.DMA,
        ]
    return pl.pallas_call(
        functools.partial(exchange_kernel, plan, n_expert, n_tensor),
        out_shape=tuple(shapes),
        in_specs=[pl.BlockSpec(memory_space=pl.ANY)] * len(arrays),
        out_specs=tuple([pl.BlockSpec(memory_space=pl.ANY)] * len(arrays)),
        scratch_shapes=scratch,
        compiler_params=pltpu.CompilerParams(collective_id=number, has_side_effects=True),
    )(*arrays)


def expert_kernel(capacity, rows_ref, cot_ref, in_ref, out_ref, back_ref, in_grad, out_grad, kept, gated, part, grad_rows):
    n_expert, rows_each, width = rows_ref.shape
    n_tensor, share = back_ref.shape[1], back_ref.shape[3] // 2
    all_rows = n_expert * rows_each
    line = lax.broadcasted_iota(jnp.int32, (rows_each, 1), 0)
    diagonal = line == lax.broadcasted_iota(jnp.int32, (rows_each, 128), 1)

    def fill(e, carry):
        rows = rows_ref[e].astype(F32)
        kept[e] = jnp.where(line < capacity, rows, 0.0).astype(BF16)
        gates = rows[capacity : capacity + 1, :128] + rows[capacity + 1 : capacity + 2, :128]
        gate = jnp.sum(jnp.where(diagonal, gates, 0.0), axis=1, keepdims=True)
        gated[e] = (gate * cot_ref[e].astype(F32)).astype(BF16)
        return carry

    lax.fori_loop(0, n_expert, fill, 0)
    inputs = kept[...].reshape(all_rows, width)
    hidden = dot(inputs, in_ref[...], ((1,), (0,)))
    normal = 0.5 * (1.0 + lax.erf(hidden * ROOT_HALF))
    active = (hidden * normal).astype(BF16)
    slope = normal + hidden * jnp.exp(-0.5 * hidden * hidden) * INV_ROOT_TAU
    part[...] = dot(active, out_ref[...], ((1,), (0,))).astype(BF16).reshape(part.shape)
    grads = gated[...].reshape(all_rows, width)
    grad_hidden = (dot(grads, out_ref[...], ((1,), (1,))) * slope).astype(BF16)
    grad_rows[...] = dot(grad_hidden, in_ref[...], ((1,), (1,))).astype(BF16).reshape(part.shape)

    def send(e, carry):
        forward, backward = part[e], grad_rows[e]
        dots = jnp.sum(forward.astype(F32) * cot_ref[e].astype(F32), axis=1, keepdims=True)
        row = jnp.sum(jnp.where(diagonal, dots, 0.0), axis=0, keepdims=True)
        high = row.astype(BF16).astype(F32)
        blank = jnp.zeros((1, 2 * share - 128), F32)
        high, low = [jnp.concatenate([x, blank], axis=1) for x in (high, row - high)]
        for g in range(n_tensor):
            span = slice(g * share, (g + 1) * share)
            body = jnp.concatenate([forward[:, span], backward[:, span]], axis=1).astype(F32)
            body = jnp.where(line == capacity, high, jnp.where(line == capacity + 1, low, body))
            back_ref[e, g] = body.astype(BF16)
        return carry

    lax.fori_loop(0, n_expert, send, 0)
    out_grad[...] = dot(active, grads, ((0,), (0,)))
    in_grad[...] = dot(inputs, grad_hidden, ((0,), (0,)))


def run_expert(rows, cot_rows, w_in, w_out, capacity, n_tensor):
    n_expert, rows_each, width = rows.shape
    share = width // n_tensor
    inner = w_in.shape[1]
    vmem = pl.BlockSpec(memory_space=pltpu.VMEM)
    return pl.pallas_call(
        functools.partial(expert_kernel, capacity),
        out_shape=(
            jax.ShapeDtypeStruct((n_expert, n_tensor, rows_each, 2 * share), BF16),
            jax.ShapeDtypeStruct((width, inner), F32),
            jax.ShapeDtypeStruct((inner, width), F32),
        ),
        in_specs=[vmem] * 4,
        out_specs=(vmem,) * 3,
        scratch_shapes=[pltpu.VMEM((n_expert, rows_each, width), BF16)] * 4,
        compiler_params=pltpu.CompilerParams(vmem_limit_bytes=48 << 20),
    )(rows, cot_rows, w_in, w_out)


def diagonal_sums(grid):
    heads_here, length, _ = grid.shape
    flipped = grid[:, :, ::-1]
    padded = jnp.concatenate([flipped, jnp.zeros_like(flipped)], axis=2).reshape(heads_here, -1)
    window = lax.slice_in_dim(padded, length - 1, length - 1 + length * (2 * length - 1), axis=1)
    window = window.reshape(heads_here, length, 2 * length - 1)
    return jnp.sum(window[:, :, :length], axis=1)


def spread_diagonals(rows):
    heads_here, length = rows.shape
    period = jnp.concatenate(
        [rows[:, :1], jnp.zeros((heads_here, length), F32), rows[:, :0:-1]], axis=1
    )
    flat = jnp.tile(period, (1, length))[:, : length * (2 * length - 1)]
    return flat.reshape(heads_here, length, 2 * length - 1)[:, :, :length]


def two_parts(values):
    high = lax.reduce_precision(values, 8, 7)
    return high.astype(BF16), (values - high).astype(BF16)


def dot(a, b, dims):
    return lax.dot_general(a, b, (dims, ((), ())), preferred_element_type=F32)


def per_device(
    tokens,
    cotangent,
    attn_gain,
    qkv_weight,
    out_weight,
    bias_table,
    ffn_gain,
    router_weight,
    expert_in,
    expert_out,
    routes,
    buckets,
):
    n_expert, n_tensor = lax.axis_size("expert"), lax.axis_size("tensor")
    tensor_index = lax.axis_index("tensor")
    seq_len, share = tokens.shape
    width = share * n_tensor
    heads_here = bias_table.shape[1]
    local = qkv_weight.shape[2]
    head_size = local // heads_here
    experts = router_weight.shape[1]
    top_count = routes.shape[1]
    capacity = 4 * top_count * seq_len // (3 * experts)
    rows_each = -(-(capacity + 2) // 16) * 16
    all_rows = experts * rows_each

    block = width // n_expert
    gathers = block % 16 == 0
    both, *share_rows = exchange(
        0,
        ("tensor", "whole", jnp.concatenate([tokens, cotangent], axis=1)),
        *([("expert", "relay", tokens)] if gathers else []),
    )
    both = both.transpose(1, 0, 2)
    inputs = both[:, :, :share].reshape(seq_len, width).astype(F32)
    whole_cot = both[:, :, share:].reshape(seq_len, width)
    grad_out = whole_cot.astype(F32)

    expert_ids = jnp.arange(experts, dtype=jnp.int32)
    chosen = routes[:, :, None] == expert_ids[None, None, :]
    paired = routes.reshape(-1)
    pair_hot = (paired[:, None] == expert_ids[None, :]).astype(F32)
    order = jnp.arange(seq_len * top_count, dtype=jnp.int32)
    before = (order[:, None] > order[None, :]).astype(BF16)
    earlier = dot(before, pair_hot.astype(BF16), ((1,), (0,)))
    slots = jnp.sum(earlier * pair_hot, axis=-1).astype(jnp.int32)
    target_pairs = (paired * rows_each + slots).reshape(seq_len, top_count)
    back_pairs = (paired * (n_tensor * rows_each) + slots).reshape(seq_len, top_count)
    columns = jnp.arange(all_rows, dtype=jnp.int32)
    picks = [target_pairs[:, k : k + 1] == columns[None, :] for k in range(top_count)]
    pick_all = sum([pick.astype(BF16) for pick in picks])
    cot_rows = dot(pick_all, whole_cot, ((0,), (0,))).astype(BF16)

    r_first = lax.rsqrt(jnp.mean(inputs * inputs, axis=-1, keepdims=True) + EPSILON)
    gain = attn_gain.astype(F32)
    normed = (inputs * r_first * gain).astype(BF16)
    projected = jnp.einsum("td,cdf->ctf", normed, qkv_weight, preferred_element_type=F32).astype(BF16)
    queries = projected[0].reshape(seq_len, heads_here, head_size)
    keys_here = projected[1].reshape(seq_len, heads_here, head_size)
    values_here = projected[2].reshape(seq_len, heads_here, head_size)
    position = jnp.arange(seq_len, dtype=jnp.int32)
    causal = position[:, None] >= position[None, :]
    bucket_hot = (
        buckets[:, None] == jnp.arange(bias_table.shape[0], dtype=jnp.int32)[None, :]
    ).astype(F32)
    bias_rows = jnp.einsum("bh,tb->ht", bias_table, bucket_hot, precision=PRECISE)
    full_bias = spread_diagonals(bias_rows)
    raw_scores = (
        jnp.einsum("qhd,khd->hqk", queries, keys_here, preferred_element_type=F32) * 0.125 + full_bias
    )
    scores = jnp.where(causal[None], raw_scores, -1e30)
    row_max = jnp.max(scores, axis=-1, keepdims=True)
    powers = jnp.exp(scores - row_max)
    soft = powers / jnp.sum(powers, axis=-1, keepdims=True)
    weights = soft.astype(BF16)
    context = jnp.einsum("hqk,khd->qhd", weights, values_here, preferred_element_type=F32)
    context = context.astype(BF16).reshape(seq_len, local)

    whole_context, whole_out, cot_recv = exchange(
        1,
        ("tensor", "relay", context),
        ("tensor", "relay", out_weight),
        ("expert", "split", cot_rows.reshape(n_expert, rows_each, width)),
    )
    attended = dot(
        whole_context.transpose(1, 0, 2).reshape(seq_len, width),
        whole_out.reshape(width, width),
        ((1,), (0,)),
    )
    residual = inputs + attended
    r_second = lax.rsqrt(jnp.mean(residual * residual, axis=-1, keepdims=True) + EPSILON)
    ffn_in = (residual * r_second * ffn_gain.astype(F32)).astype(BF16)
    router_probs = jax.nn.softmax(dot(ffn_in, router_weight, ((1,), (0,))), axis=-1)
    gate_values = jnp.sum(jnp.where(chosen, router_probs[:, None, :], 0.0), axis=-1)
    slot_gate = sum(
        [
            jnp.sum(jnp.where(picks[k], gate_values[:, k : k + 1], 0.0), axis=0)
            for k in range(top_count)
        ]
    ).reshape(n_expert, rows_each)
    line = jnp.arange(rows_each, dtype=jnp.int32)

    def add_lines(body, values):
        extra = body.ndim - 3
        high, low = [
            jnp.pad(part, ((0, 0), (0, body.shape[-1] - rows_each))).reshape(
                (n_expert,) + (1,) * (extra + 1) + (body.shape[-1],)
            )
            for part in two_parts(values)
        ]
        at = line[:, None]
        return jnp.where(at == capacity, high, jnp.where(at == capacity + 1, low, body))

    def read_lines(body):
        return (
            body[..., capacity, :rows_each].astype(F32)
            + body[..., capacity + 1, :rows_each].astype(F32)
        )

    send_rows = dot(pick_all, ffn_in, ((0,), (0,))).astype(BF16).reshape(n_expert, rows_each, width)
    received, *all_tokens = exchange(
        2,
        ("expert", "split", add_lines(send_rows, slot_gate)),
        *[("tensor", "relay", rows.reshape(n_expert * seq_len, share)) for rows in share_rows],
    )
    back, expert_in_grad, expert_out_grad = run_expert(
        received, cot_recv, expert_in[0], expert_out[0], capacity, n_tensor
    )
    expert_in_grad, expert_out_grad = expert_in_grad[None], expert_out_grad[None]
    (returned,) = exchange(3, ("all", "split", back))
    slot_dots = jnp.sum(read_lines(returned), axis=1).reshape(1, all_rows)
    grad_gates = jnp.stack(
        [jnp.sum(jnp.where(picks[k], slot_dots, 0.0), axis=-1) for k in range(top_count)], axis=-1
    )
    places = jnp.arange(n_tensor * all_rows, dtype=jnp.int32)
    group_start = places - (places // rows_each % n_tensor) * rows_each
    back_pick = jnp.concatenate(
        [back_pairs[:, k : k + 1] == group_start[None, :] for k in range(top_count)], axis=0
    ).astype(BF16)
    picked = dot(back_pick, returned.reshape(n_tensor * all_rows, 2 * share), ((1,), (0,)))
    picked = picked.reshape(top_count, seq_len, 2 * share)
    expert_share = sum([gate_values[:, k : k + 1] * picked[k, :, :share] for k in range(top_count)])
    residual_share = lax.dynamic_slice_in_dim(residual, tensor_index * share, share, 1)
    mixed = (residual_share + expert_share).astype(BF16)

    grad_ffn_share = jnp.sum(picked[:, :, share:], axis=0).astype(BF16)
    (grad_ffn_experts,) = exchange(4, ("tensor", "whole", grad_ffn_share))
    grad_ffn_experts = grad_ffn_experts.transpose(1, 0, 2).reshape(seq_len, width).astype(F32)
    grad_probs = jnp.sum(jnp.where(chosen, grad_gates[:, :, None], 0.0), axis=1)
    grad_logits = (
        router_probs * (grad_probs - jnp.sum(router_probs * grad_probs, axis=-1, keepdims=True))
    ).astype(BF16)
    router_grad = dot(grad_logits, ffn_in, ((0,), (0,)))
    grad_ffn_in = grad_ffn_experts + dot(grad_logits, router_weight, ((1,), (1,)))
    ffn_gain_grad = jnp.sum(grad_ffn_in * residual * r_second, axis=0)
    scaled_second = grad_ffn_in * ffn_gain.astype(F32)
    grad_residual = (
        grad_out
        + r_second * scaled_second
        - residual * r_second**3 * jnp.mean(scaled_second * residual, axis=-1, keepdims=True)
    )
    grad_attended = grad_residual.astype(BF16)
    grad_context = dot(grad_attended, out_weight, ((1,), (1,))).astype(BF16)
    grad_context = grad_context.reshape(seq_len, heads_here, head_size)
    grad_values = jnp.einsum("hqk,qhd->khd", weights, grad_context, preferred_element_type=F32)
    grad_weights = jnp.einsum("qhd,khd->hqk", grad_context, values_here, preferred_element_type=F32)
    grad_scores = (
        soft * (grad_weights - jnp.sum(soft * grad_weights, axis=-1, keepdims=True))
    ).astype(BF16)
    grad_queries = jnp.einsum("hqk,khd->qhd", grad_scores, keys_here, preferred_element_type=F32) * 0.125
    grad_keys = jnp.einsum("hqk,qhd->khd", grad_scores, queries, preferred_element_type=F32) * 0.125
    distance_grad = diagonal_sums(grad_scores.astype(F32))
    table_grad = jnp.einsum("tb,ht->bh", bucket_hot, distance_grad, precision=PRECISE)
    grad_projected = jnp.concatenate(
        [part.astype(BF16).reshape(seq_len, local) for part in (grad_queries, grad_keys, grad_values)],
        axis=1,
    )
    qkv_flat = qkv_weight.transpose(1, 0, 2).reshape(width, 3 * local)
    grad_normed_part = dot(grad_projected, qkv_flat, ((1,), (1,)))
    out_grad = dot(grad_attended, context, ((0,), (0,)))
    attn_part = jnp.sum(grad_normed_part * inputs * r_first, axis=0)
    row_part = jnp.sum(grad_normed_part * attn_gain.astype(F32) * inputs, axis=-1, keepdims=True)
    row_high, row_low = two_parts(row_part)
    shares = grad_normed_part.astype(BF16).reshape(seq_len, n_tensor, share).transpose(1, 0, 2)
    pad = (-share - 2) % 128
    tail = jnp.concatenate([row_high, row_low, jnp.zeros((seq_len, pad), BF16)], axis=1)
    shares = jnp.concatenate(
        [shares, jnp.broadcast_to(tail[None], (n_tensor,) + tail.shape)], axis=2
    )
    table_line = jnp.pad(table_grad.reshape(1, -1), ((0, 0), (0, width - table_grad.size)))
    pack = jnp.concatenate([attn_part[None], ffn_gain_grad[None], table_line, router_grad], axis=0)
    pack = jnp.pad(pack, ((0, -pack.shape[0] % 16), (0, 0)))
    moves = [("expert", "relay", pack.astype(BF16)), ("tensor", "split", shares)]
    if gathers:
        pieces = out_grad.astype(BF16).reshape(n_expert, block, local)
        all_projected, packs, normed_parts, pieces = exchange(
            5, ("expert", "relay", grad_projected), *moves, ("expert", "split", pieces)
        )
        piece = jnp.sum(pieces.astype(F32), axis=0).astype(BF16)
    else:
        packs, normed_parts = exchange(5, *moves)
    pack = jnp.sum(packs.astype(F32), axis=0)
    attn_rows = jnp.pad(pack[:1], ((0, 7), (0, 0)))
    if gathers:
        pieces, attn_rows = exchange(
            6, ("expert", "relay", piece), ("tensor", "whole", attn_rows)
        )
        out_grad = pieces.reshape(width, local).astype(F32)
        all_tokens = all_tokens[0].transpose(1, 0, 2).reshape(n_expert * seq_len, width).astype(F32)
        all_r = lax.rsqrt(jnp.mean(all_tokens * all_tokens, axis=-1, keepdims=True) + EPSILON)
        all_normed = (all_tokens * all_r * gain).astype(BF16)
        all_projected = all_projected.reshape(n_expert * seq_len, 3 * local)
    else:
        (attn_rows,) = exchange(6, ("tensor", "whole", attn_rows))
        all_normed, all_projected = normed, grad_projected
    qkv_grad = jnp.stack(
        [
            dot(all_normed, all_projected[:, c * local : (c + 1) * local], ((0,), (0,)))
            for c in range(3)
        ]
    )
    if not gathers:
        out_grad, qkv_grad = lax.psum((out_grad, qkv_grad), "expert")
    attn_gain_grad = jnp.sum(attn_rows[:, 0], axis=0)
    normed_sum = jnp.sum(normed_parts.astype(F32), axis=0)
    row_mean = (normed_sum[:, share : share + 1] + normed_sum[:, share + 1 : share + 2]) / width

    def own_share(values):
        return lax.dynamic_slice_in_dim(values, tensor_index * share, share, values.ndim - 1)

    own_inputs = tokens.astype(F32)
    tokens_grad = (
        own_share(grad_residual)
        + r_first * (normed_sum[:, :share] * own_share(attn_gain.astype(F32)))
        - own_inputs * r_first**3 * row_mean
    ).astype(BF16)
    return (
        mixed,
        tokens_grad,
        attn_gain_grad,
        qkv_grad,
        out_grad.T,
        pack[2, : table_grad.size].reshape(table_grad.shape),
        pack[1],
        pack[3 : 3 + experts].T,
        expert_in_grad,
        expert_out_grad,
    )


def solution(mesh):
    placed = (
        P("expert", "tensor"),
        P("expert", "tensor"),
        P(),
        P(None, None, "tensor"),
        P("tensor", None),
        P(None, "tensor"),
        P(),
        P(),
        P("expert", None, "tensor"),
        P("expert", "tensor", None),
        P("expert", None),
        P(),
    )
    return jax.shard_map(
        per_device,
        mesh=mesh,
        in_specs=placed,
        out_specs=(
            P("expert", "tensor"),
            P("expert", "tensor"),
            P(),
            P(None, None, "tensor"),
            P("tensor", None),
            P(None, "tensor"),
            P(),
            P(),
            P("expert", None, "tensor"),
            P("expert", "tensor", None),
        ),
        check_vma=False,
    )
```
